32 devices in a mesh: slab: 2 (over y), tm: 8 (over z, x), space: 2 (over core).
Axes of the slice: x: 2, y: 2, z: 4, core: 2. Of those that a mesh axis runs over, the one named last changes fastest.
Arguments:
- snaps: float32 [128, 8192], P('tm', ('slab', 'space')), parts along dimension 1, may hold values from -6 to 6
- weights: float32 [8192], P(('slab', 'space')), parts along dimension 0, may hold values from 0.00012207031 to 0.0009765625
Outputs:
- gram: float32 [256, 128], P(('slab', 'tm', 'space')), parts along dimension 0
The draws below stay inside these ranges and needn't reach their ends.
There are 2 independent parts, one for each index of `slab`. The reference program is written for one: setup_inputs(seed, part) draws one part's arguments, and reference() takes and returns one part's arrays. A program takes and returns all parts, laid end to end along the dimension named above; each array names one. Nothing has to cross between parts.
All inputs are finite; a program needn't handle non-finite values.
Results may differ from the reference program's by a relative error of at most 0.000067.
Values sent between devices are 32-bit elements; how exact they have to be, the bound alone decides.
A program may use at most 64 MiB of HBM per device.

```python
import math
import jax
import jax.numpy as jnp
from jax import lax

CELLS = 4096
SNAPS = 128


def levels(key, shape, pieces, low, largest):
    level = 1.0
    for dim, parts in pieces:
        heights = jax.random.uniform(jax.random.fold_in(jax.random.fold_in(key, 6), dim), (parts,), jnp.float32, low / len(pieces), largest / len(pieces))
        level = level * jnp.repeat(jnp.exp(heights), shape[dim] // parts).reshape((-1,) + (1,) * (len(shape) - 1 - dim))
    return level


def gaussian(own_key, dims, spread, most, shards=(), dtype=jnp.bfloat16):
    entries = jax.random.normal(own_key, dims, jnp.float32) * spread
    if len(shards) > 0:
        entries = levels(own_key, dims, shards, -0.22, 0.18) * entries
    return jnp.clip(entries, min=-most, max=most).astype(dtype)


def setup_inputs(seed: int = 0, part: int = 0) -> dict:
    splits = jax.random.split(jax.random.key(seed), 3)
    own_keys = jax.random.split(jax.random.fold_in(splits[2], part), 3)
    snaps = gaussian(own_keys[0], (SNAPS, CELLS), 1.0, 6.0, ((0, 8), (1, 2)), jnp.float32)
    weights = jnp.clip(jnp.exp(math.log(0.0009765625) - 2.0794415 * jax.random.uniform(own_keys[1], (CELLS,), jnp.float32) ** levels(own_keys[1], (CELLS,), ((0, 2),), -0.2, 0.2)), 0.00012207031, 0.0009765625)
    return {"snaps": snaps, "weights": weights}


def reference(snaps, weights):
    weighted = snaps * weights[None, :]
    return jnp.dot(weighted, snaps.T, precision=lax.Precision.HIGHEST, preferred_element_type=jnp.float32)
```

```python
import functools

import jax
import jax.numpy as jnp
from jax import lax
from jax.experimental import pallas as pl
from jax.experimental.pallas import tpu as pltpu
from jax.sharding import PartitionSpec as P

MESH = pl.DeviceIdType.MESH
LANES = 128


def exchange_kernel(n, spaces, snaps_ref, weights_ref, out_ref, block, gram, landed, own_sem, send_one, recv_one, send_two, recv_two):
    t, s = lax.axis_index("tm"), lax.axis_index("space")
    me = t * spaces + s
    everyone = n * spaces
    depth = snaps_ref.shape[0]
    cells = snaps_ref.shape[1] // n
    rows = depth // spaces

    barrier = pltpu.get_barrier_semaphore()
    for d in range(1, everyone):
        q = lax.rem(me + d, everyone)
        pl.semaphore_signal(
            barrier,
            inc=1,
            device_id={"tm": lax.div(q, spaces), "space": lax.rem(q, spaces)},
            device_id_type=MESH,
        )

    def columns(owner):
        return pl.ds(pl.multiple_of(owner * cells, cells), cells)

    my_rows = block.at[pl.ds(pl.multiple_of(t * depth, depth), depth), :]
    own = pltpu.make_async_copy(snaps_ref.at[:, columns(t)], my_rows, own_sem)
    own.start()
    pl.semaphore_wait(barrier, everyone - 1)

    first = []
    for d in range(1, n):
        to = lax.rem(t + d, n)
        copy = pltpu.make_async_remote_copy(
            src_ref=snaps_ref.at[:, columns(to)],
            dst_ref=my_rows,
            send_sem=send_one.at[d],
            recv_sem=recv_one.at[d],
            device_id={"tm": to},
            device_id_type=MESH,
        )
        copy.start()
        first.append(copy)
    own.wait()
    for copy in first:
        copy.wait_recv()

    pieces = cells // LANES
    weights = weights_ref[pl.ds(t * pieces, pieces), :]
    data = block[...]
    weighted = jnp.concatenate(
        [data[:, k * LANES : (k + 1) * LANES] * weights[k : k + 1, :] for k in range(pieces)], axis=1
    )
    gram[...] = lax.dot_general(
        weighted,
        data,
        (((1,), (1,)), ((), ())),
        precision=lax.Precision.HIGHEST,
        preferred_element_type=jnp.float32,
    )

    second = []
    for d in range(1, everyone):
        q = lax.rem(me + d, everyone)
        copy = pltpu.make_async_remote_copy(
            src_ref=gram.at[pl.ds(pl.multiple_of(q * rows, rows), rows), :],
            dst_ref=landed.at[d],
            send_sem=send_two.at[d],
            recv_sem=recv_two.at[d],
            device_id={"tm": lax.div(q, spaces), "space": lax.rem(q, spaces)},
            device_id_type=MESH,
        )
        copy.start()
        second.append(copy)
    total = gram[pl.ds(pl.multiple_of(me * rows, rows), rows), :]
    for d, copy in enumerate(second, 1):
        copy.wait_recv()
        total = total + landed[d]
    out_ref[...] = total
    for copy in first + second:
        copy.wait_send()


def by_exchange(n, spaces, snaps, weights):
    depth, local = snaps.shape
    cells = local // n
    everyone = n * spaces
    order = n * depth
    rows = depth // spaces
    return pl.pallas_call(
        functools.partial(exchange_kernel, n, spaces),
        out_shape=jax.ShapeDtypeStruct((rows, order), jnp.float32),
        in_specs=[pl.BlockSpec(memory_space=pl.ANY), pl.BlockSpec(memory_space=pltpu.VMEM)],
        out_specs=pl.BlockSpec(memory_space=pltpu.VMEM),
        scratch_shapes=[
            pltpu.VMEM((order, cells), jnp.float32),
            pltpu.VMEM((order, order), jnp.float32),
            pltpu.VMEM((everyone, rows, order), jnp.float32),
            pltpu.SemaphoreType.DMA,
            pltpu.SemaphoreType.DMA((n,)),
            pltpu.SemaphoreType.DMA((n,)),
            pltpu.SemaphoreType.DMA((everyone,)),
            pltpu.SemaphoreType.DMA((everyone,)),
        ],
        compiler_params=pltpu.CompilerParams(collective_id=0, has_side_effects=True),
        cost_estimate=pl.CostEstimate(
            flops=12 * order * order * cells, bytes_accessed=4 * depth * local, transcendentals=0
        ),
    )(snaps, weights.reshape(local // LANES, LANES))


def from_behind(block, axis, distance):
    devices = range(lax.axis_size(axis))
    route = [((i - distance) % len(devices), i) for i in devices]
    return lax.ppermute(block, axis, route)


def by_ring(snaps, weights):
    snap_cols = snaps.shape[0]
    half_rows = snap_cols // 2
    cycle_size = lax.axis_size("tm")
    position = lax.axis_index("tm")
    halfway = cycle_size // 2
    weighted = snaps * weights[None, :]

    def product_tile(block_now):
        return lax.dot_general(
            weighted,
            block_now,
            (((1,), (1,)), ((), ())),
            precision=lax.Precision.HIGHEST,
            preferred_element_type=jnp.float32,
        )

    def advance(block_now):
        return from_behind(block_now, "tm", -1)

    partials = jnp.zeros((halfway + 1, snap_cols, snap_cols), jnp.float32)
    partials = lax.dynamic_update_index_in_dim(partials, product_tile(snaps), 0, 0)

    def advance_four(step_index, carry):
        block_now, partials = carry
        for offset_step in range(4):
            block_now = advance(block_now)
            partials = lax.dynamic_update_index_in_dim(
                partials, product_tile(block_now), 4 * step_index + offset_step + 1, 0
            )
        return (block_now, partials)

    block_now, partials = lax.fori_loop(0, halfway // 4, advance_four, (snaps, partials))
    offsets = jnp.arange(halfway + 1, dtype=jnp.int32)
    keep_last = jnp.where((offsets == halfway) & (position >= halfway), 0.0, 1.0).astype(
        jnp.float32
    )
    partials = partials * keep_last[:, None, None]
    summed = lax.psum_scatter(partials, "space", scatter_dimension=1, tiled=True)
    padding_up = jnp.zeros((cycle_size - halfway - 1, half_rows, snap_cols), jnp.float32)
    upper = jnp.roll(jnp.concatenate([summed, padding_up], axis=0), position, axis=0)
    keep_mirror = jnp.where(offsets > 0, 1.0, 0.0).astype(jnp.float32)
    flipped = jnp.swapaxes(summed, 1, 2) * keep_mirror[:, None, None]
    padding_down = jnp.zeros((cycle_size - halfway - 1, snap_cols, half_rows), jnp.float32)
    outgoing = jnp.roll(jnp.concatenate([flipped, padding_down], axis=0), position, axis=0)
    incoming = lax.all_to_all(
        lax.all_to_all(outgoing, "tm", split_axis=0, concat_axis=0, tiled=True),
        "space",
        split_axis=1,
        concat_axis=2,
        tiled=True,
    )
    panel = upper + incoming
    return jnp.transpose(panel, (1, 0, 2)).reshape(half_rows, cycle_size * snap_cols)


def solution(mesh):
    n, spaces = mesh.shape["tm"], mesh.shape["space"]

    def on_device(snaps, weights):
        depth, local = snaps.shape
        if local % (n * LANES) == 0 and depth % (8 * spaces) == 0:
            return by_exchange(n, spaces, snaps, weights)
        return by_ring(snaps, weights)

    return jax.shard_map(
        on_device,
        mesh=mesh,
        in_specs=(P("tm", ("slab", "space")), P(("slab", "space"))),
        out_specs=P(("slab", "tm", "space"), None),
        check_vma=False,
    )
```

```python
import functools

import jax
import jax.numpy as jnp
from jax import lax
from jax.experimental import pallas as pl
from jax.experimental.pallas import tpu as pltpu
from jax.sharding import PartitionSpec as P

MESH = pl.DeviceIdType.MESH
LANES = 128


def exchange_kernel(
    n, spaces, makers, snaps_ref, weights_ref, out_ref, block, scale, gram, landed,
    own_sem, ready, send_one, recv_one, send_two, recv_two,
):
    t, s = lax.axis_index("tm"), lax.axis_index("space")
    me = t * spaces + s
    everyone, every_maker = n * spaces, makers * spaces
    depth = snaps_ref.shape[0]
    cells = snaps_ref.shape[1] // makers
    rows = depth // spaces
    makes = t < makers

    def device(q):
        return {"tm": q // spaces, "space": q % spaces}

    def columns(k):
        return pl.ds(k * cells, cells)

    barrier = pltpu.get_barrier_semaphore()
    for q in range(everyone):

        @pl.when(makes & (me != q))
        def _():
            pl.semaphore_signal(barrier, inc=1, device_id=device(q), device_id_type=MESH)

    my_rows = block.at[pl.ds(pl.multiple_of(t * depth, depth), depth), :]
    own_columns = pl.ds(pl.multiple_of(lax.rem(t, makers) * cells, cells), cells)
    own = pltpu.make_async_copy(snaps_ref.at[:, own_columns], my_rows, own_sem.at[0])
    load = pltpu.make_async_copy(weights_ref, scale, own_sem.at[1])

    @pl.when(makes)
    def _():
        own.start()
        load.start()

    pl.semaphore_wait(barrier, jnp.where(makes, every_maker - 1, every_maker))

    def first(k):
        return pltpu.make_async_remote_copy(
            src_ref=snaps_ref.at[:, columns(k)],
            dst_ref=my_rows,
            send_sem=send_one.at[k],
            recv_sem=recv_one.at[lax.rem(t - k + n, n)],
            device_id={"tm": k},
            device_id_type=MESH,
        )

    for k in range(makers):

        @pl.when(t != k)
        def _():
            first(k).start()

    for k in range(makers):
        for other in range(1, spaces):
            pl.semaphore_signal(
                ready,
                inc=1,
                device_id={"tm": k, "space": lax.rem(s + other, spaces)},
                device_id_type=MESH,
            )

    def second(q):
        return pltpu.make_async_remote_copy(
            src_ref=gram.at[pl.ds(q * rows, rows), :],
            dst_ref=landed.at[me],
            send_sem=send_two.at[q],
            recv_sem=recv_two.at[me],
            device_id=device(q),
            device_id_type=MESH,
        )

    @pl.when(makes)
    def _():
        own.wait()
        load.wait()
        for d in range(1, n):
            source = lax.rem(t + d, n)
            theirs = block.at[pl.ds(pl.multiple_of(source * depth, depth), depth), :]
            pltpu.make_async_copy(theirs, theirs, recv_one.at[d]).wait()
        pieces = cells // LANES
        weights = scale[pl.ds(t * pieces, pieces), :]
        data = block[...]
        weighted = jnp.concatenate(
            [data[:, k * LANES : (k + 1) * LANES] * weights[k : k + 1, :] for k in range(pieces)],
            axis=1,
        )
        gram[...] = lax.dot_general(
            weighted,
            data,
            (((1,), (1,)), ((), ())),
            precision=lax.Precision.HIGHEST,
            preferred_element_type=jnp.float32,
        )
        pl.semaphore_wait(ready, (spaces - 1) * n)
        for q in range(everyone):

            @pl.when(me != q)
            def _():
                second(q).start()

        landed[me] = gram[pl.ds(pl.multiple_of(me * rows, rows), rows), :]

    for m in range(every_maker):

        @pl.when(me != m)
        def _():
            pltpu.make_async_copy(landed.at[m], landed.at[m], recv_two.at[m]).wait()

    total = landed[0]
    for m in range(1, every_maker):
        total = total + landed[m]
    out_ref[...] = total

    for k in range(makers):

        @pl.when(t != k)
        def _():
            first(k).wait_send()

    @pl.when(makes)
    def _():
        for q in range(everyone):

            @pl.when(me != q)
            def _():
                second(q).wait_send()


def by_exchange(n, spaces, makers, snaps, weights):
    depth, local = snaps.shape
    cells = local // makers
    everyone, every_maker = n * spaces, makers * spaces
    order = n * depth
    rows = depth // spaces
    return pl.pallas_call(
        functools.partial(exchange_kernel, n, spaces, makers),
        out_shape=jax.ShapeDtypeStruct((rows, order), jnp.float32),
        in_specs=[pl.BlockSpec(memory_space=pl.ANY)] * 2,
        out_specs=pl.BlockSpec(memory_space=pltpu.VMEM),
        scratch_shapes=[
            pltpu.VMEM((order, cells), jnp.float32),
            pltpu.VMEM((local // LANES, LANES), jnp.float32),
            pltpu.VMEM((order, order), jnp.float32),
            pltpu.VMEM((every_maker, rows, order), jnp.float32),
            pltpu.SemaphoreType.DMA((2,)),
            pltpu.SemaphoreType.REGULAR,
            pltpu.SemaphoreType.DMA((makers,)),
            pltpu.SemaphoreType.DMA((n,)),
            pltpu.SemaphoreType.DMA((everyone,)),
            pltpu.SemaphoreType.DMA((every_maker,)),
        ],
        compiler_params=pltpu.CompilerParams(collective_id=0, has_side_effects=True),
        cost_estimate=pl.CostEstimate(
            flops=12 * order * order * cells, bytes_accessed=4 * depth * local, transcendentals=0
        ),
    )(snaps, weights.reshape(local // LANES, LANES))


def from_behind(block, axis, distance):
    devices = range(lax.axis_size(axis))
    route = [((i - distance) % len(devices), i) for i in devices]
    return lax.ppermute(block, axis, route)


def by_ring(snaps, weights):
    snap_cols = snaps.shape[0]
    half_rows = snap_cols // 2
    cycle_size = lax.axis_size("tm")
    position = lax.axis_index("tm")
    halfway = cycle_size // 2
    weighted = snaps * weights[None, :]

    def product_tile(block_now):
        return lax.dot_general(
            weighted,
            block_now,
            (((1,), (1,)), ((), ())),
            precision=lax.Precision.HIGHEST,
            preferred_element_type=jnp.float32,
        )

    def advance(block_now):
        return from_behind(block_now, "tm", -1)

    partials = jnp.zeros((halfway + 1, snap_cols, snap_cols), jnp.float32)
    partials = lax.dynamic_update_index_in_dim(partials, product_tile(snaps), 0, 0)

    def advance_four(step_index, carry):
        block_now, partials = carry
        for offset_step in range(4):
            block_now = advance(block_now)
            partials = lax.dynamic_update_index_in_dim(
                partials, product_tile(block_now), 4 * step_index + offset_step + 1, 0
            )
        return (block_now, partials)

    block_now, partials = lax.fori_loop(0, halfway // 4, advance_four, (snaps, partials))
    offsets = jnp.arange(halfway + 1, dtype=jnp.int32)
    keep_last = jnp.where((offsets == halfway) & (position >= halfway), 0.0, 1.0).astype(
        jnp.float32
    )
    partials = partials * keep_last[:, None, None]
    summed = lax.psum_scatter(partials, "space", scatter_dimension=1, tiled=True)
    padding_up = jnp.zeros((cycle_size - halfway - 1, half_rows, snap_cols), jnp.float32)
    upper = jnp.roll(jnp.concatenate([summed, padding_up], axis=0), position, axis=0)
    keep_mirror = jnp.where(offsets > 0, 1.0, 0.0).astype(jnp.float32)
    flipped = jnp.swapaxes(summed, 1, 2) * keep_mirror[:, None, None]
    padding_down = jnp.zeros((cycle_size - halfway - 1, snap_cols, half_rows), jnp.float32)
    outgoing = jnp.roll(jnp.concatenate([flipped, padding_down], axis=0), position, axis=0)
    incoming = lax.all_to_all(
        lax.all_to_all(outgoing, "tm", split_axis=0, concat_axis=0, tiled=True),
        "space",
        split_axis=1,
        concat_axis=2,
        tiled=True,
    )
    panel = upper + incoming
    return jnp.transpose(panel, (1, 0, 2)).reshape(half_rows, cycle_size * snap_cols)


def solution(mesh):
    n, spaces = mesh.shape["tm"], mesh.shape["space"]
    makers = max(n // 2, 1)

    def on_device(snaps, weights):
        depth, local = snaps.shape
        if local % (makers * LANES) == 0 and depth % (8 * spaces) == 0:
            return by_exchange(n, spaces, makers, snaps, weights)
        return by_ring(snaps, weights)

    return jax.shard_map(
        on_device,
        mesh=mesh,
        in_specs=(P("tm", ("slab", "space")), P(("slab", "space"))),
        out_specs=P(("slab", "tm", "space"), None),
        check_vma=False,
    )
```

```python
import functools

import jax
import jax.numpy as jnp
from jax import lax
from jax.experimental import pallas as pl
from jax.experimental.pallas import tpu as pltpu
from jax.sharding import PartitionSpec as P

MESH = pl.DeviceIdType.MESH
LANES = 128


def shares_of(n, pieces):
    makers = n // 2 + 1
    return tuple((pieces + k) // makers for k in range(makers))


def order_of(makers):
    return list(range(makers))[1::2][::-1] + list(range(makers))[0::2][::-1]


def exchange_kernel(
    n, spaces, shares, snaps_ref, weights_ref, landed, block, scale, gram,
    own_sem, ready, send_one, recv_one, send_two, recv_two,
):
    t, s = lax.axis_index("tm"), lax.axis_index("space")
    me = t * spaces + s
    makers = len(shares)
    starts = [sum(shares[:k]) for k in range(makers)]
    everyone, every_maker = n * spaces, makers * spaces
    depth = snaps_ref.shape[0]
    rows = depth // spaces
    makes = t < makers

    def device(q):
        return {"tm": q // spaces, "space": q % spaces}

    def columns(k):
        return pl.ds(starts[k] * LANES, shares[k] * LANES)

    def by_share(work):
        for share in sorted(set(shares)):
            mine = [k for k in range(makers) if shares[k] == share]
            is_mine = functools.reduce(jnp.logical_or, [t == k for k in mine])
            pl.when(is_mine)(functools.partial(work, share))

    start = sum(jnp.where(t == k, starts[k], 0) for k in range(makers))

    barrier = pltpu.get_barrier_semaphore()
    for q in range(everyone):

        @pl.when(makes & (me != q))
        def _():
            pl.semaphore_signal(barrier, inc=1, device_id=device(q), device_id_type=MESH)

    def rows_of(source, share):
        return block.at[pl.ds(pl.multiple_of(source * depth, depth), depth), pl.ds(0, share * LANES)]

    def own(share):
        columns = pl.ds(pl.multiple_of(start * LANES, LANES), share * LANES)
        return pltpu.make_async_copy(snaps_ref.at[:, columns], rows_of(t, share), own_sem.at[0])

    load = pltpu.make_async_copy(weights_ref, scale, own_sem.at[1])

    @by_share
    def _(share):
        own(share).start()
        load.start()

    pl.semaphore_wait(barrier, jnp.where(makes, every_maker - 1, every_maker))

    def first(k):
        return pltpu.make_async_remote_copy(
            src_ref=snaps_ref.at[:, columns(k)],
            dst_ref=rows_of(t, shares[k]),
            send_sem=send_one.at[k],
            recv_sem=recv_one.at[lax.rem(t - k + n, n)],
            device_id={"tm": k},
            device_id_type=MESH,
        )

    for k in order_of(makers):

        @pl.when(t != k)
        def _():
            first(k).start()

    for k in range(makers):
        for other in range(1, spaces):
            pl.semaphore_signal(
                ready,
                inc=1,
                device_id={"tm": k, "space": lax.rem(s + other, spaces)},
                device_id_type=MESH,
            )

    def second(q):
        return pltpu.make_async_remote_copy(
            src_ref=gram.at[pl.ds(q * rows, rows), :],
            dst_ref=landed.at[me],
            send_sem=send_two.at[q],
            recv_sem=recv_two.at[me],
            device_id=device(q),
            device_id_type=MESH,
        )

    @by_share
    def _(share):
        own(share).wait()
        load.wait()
        for d in range(1, n):
            theirs = rows_of(lax.rem(t + d, n), share)
            pltpu.make_async_copy(theirs, theirs, recv_one.at[d]).wait()
        weights = scale[pl.ds(start, share), :]
        data = block[:, 0 : share * LANES]
        weighted = jnp.concatenate(
            [data[:, k * LANES : (k + 1) * LANES] * weights[k : k + 1, :] for k in range(share)],
            axis=1,
        )
        gram[...] = lax.dot_general(
            weighted,
            data,
            (((1,), (1,)), ((), ())),
            precision=lax.Precision.HIGHEST,
            preferred_element_type=jnp.float32,
        )

    @pl.when(makes)
    def _():
        pl.semaphore_wait(ready, (spaces - 1) * n)
        for q in range(everyone):

            @pl.when(me != q)
            def _():
                second(q).start()

        keep = pltpu.make_async_copy(gram.at[pl.ds(pl.multiple_of(me * rows, rows), rows), :], landed.at[me], own_sem.at[0])
        keep.start()
        keep.wait()

    for m in range(every_maker):

        @pl.when(me != m)
        def _():
            pltpu.make_async_copy(landed.at[m], landed.at[m], recv_two.at[m]).wait()

    for k in range(makers):

        @pl.when(t != k)
        def _():
            first(k).wait_send()

    @pl.when(makes)
    def _():
        for q in range(everyone):

            @pl.when(me != q)
            def _():
                second(q).wait_send()


def by_exchange(n, spaces, shares, snaps, weights):
    depth, local = snaps.shape
    makers, cells = len(shares), max(shares) * LANES
    everyone, every_maker = n * spaces, makers * spaces
    order = n * depth
    rows = depth // spaces
    tiles = pl.pallas_call(
        functools.partial(exchange_kernel, n, spaces, shares),
        out_shape=jax.ShapeDtypeStruct((every_maker, rows, order), jnp.float32),
        in_specs=[pl.BlockSpec(memory_space=pl.ANY)] * 2,
        out_specs=pl.BlockSpec(memory_space=pl.ANY),
        scratch_shapes=[
            pltpu.VMEM((order, cells), jnp.float32),
            pltpu.VMEM((local // LANES, LANES), jnp.float32),
            pltpu.VMEM((order, order), jnp.float32),
            pltpu.SemaphoreType.DMA((2,)),
            pltpu.SemaphoreType.REGULAR,
            pltpu.SemaphoreType.DMA((makers,)),
            pltpu.SemaphoreType.DMA((n,)),
            pltpu.SemaphoreType.DMA((everyone,)),
            pltpu.SemaphoreType.DMA((every_maker,)),
        ],
        compiler_params=pltpu.CompilerParams(collective_id=0, has_side_effects=True),
        cost_estimate=pl.CostEstimate(
            flops=12 * order * order * cells, bytes_accessed=4 * depth * local, transcendentals=0
        ),
    )(snaps, weights.reshape(local // LANES, LANES))
    return jnp.sum(tiles, axis=0)


def from_behind(block, axis, distance):
    devices = range(lax.axis_size(axis))
    route = [((i - distance) % len(devices), i) for i in devices]
    return lax.ppermute(block, axis, route)


def by_ring(snaps, weights):
    snap_cols = snaps.shape[0]
    half_rows = snap_cols // 2
    cycle_size = lax.axis_size("tm")
    position = lax.axis_index("tm")
    halfway = cycle_size // 2
    weighted = snaps * weights[None, :]

    def product_tile(block_now):
        return lax.dot_general(
            weighted,
            block_now,
            (((1,), (1,)), ((), ())),
            precision=lax.Precision.HIGHEST,
            preferred_element_type=jnp.float32,
        )

    def advance(block_now):
        return from_behind(block_now, "tm", -1)

    partials = jnp.zeros((halfway + 1, snap_cols, snap_cols), jnp.float32)
    partials = lax.dynamic_update_index_in_dim(partials, product_tile(snaps), 0, 0)

    def advance_four(step_index, carry):
        block_now, partials = carry
        for offset_step in range(4):
            block_now = advance(block_now)
            partials = lax.dynamic_update_index_in_dim(
                partials, product_tile(block_now), 4 * step_index + offset_step + 1, 0
            )
        return (block_now, partials)

    block_now, partials = lax.fori_loop(0, halfway // 4, advance_four, (snaps, partials))
    offsets = jnp.arange(halfway + 1, dtype=jnp.int32)
    keep_last = jnp.where((offsets == halfway) & (position >= halfway), 0.0, 1.0).astype(
        jnp.float32
    )
    partials = partials * keep_last[:, None, None]
    summed = lax.psum_scatter(partials, "space", scatter_dimension=1, tiled=True)
    padding_up = jnp.zeros((cycle_size - halfway - 1, half_rows, snap_cols), jnp.float32)
    upper = jnp.roll(jnp.concatenate([summed, padding_up], axis=0), position, axis=0)
    keep_mirror = jnp.where(offsets > 0, 1.0, 0.0).astype(jnp.float32)
    flipped = jnp.swapaxes(summed, 1, 2) * keep_mirror[:, None, None]
    padding_down = jnp.zeros((cycle_size - halfway - 1, snap_cols, half_rows), jnp.float32)
    outgoing = jnp.roll(jnp.concatenate([flipped, padding_down], axis=0), position, axis=0)
    incoming = lax.all_to_all(
        lax.all_to_all(outgoing, "tm", split_axis=0, concat_axis=0, tiled=True),
        "space",
        split_axis=1,
        concat_axis=2,
        tiled=True,
    )
    panel = upper + incoming
    return jnp.transpose(panel, (1, 0, 2)).reshape(half_rows, cycle_size * snap_cols)


def solution(mesh):
    n, spaces = mesh.shape["tm"], mesh.shape["space"]

    def on_device(snaps, weights):
        depth, local = snaps.shape
        shares = shares_of(n, local // LANES)
        if local % LANES == 0 and min(shares) > 0 and depth % (8 * spaces) == 0:
            return by_exchange(n, spaces, shares, snaps, weights)
        return by_ring(snaps, weights)

    return jax.shard_map(
        on_device,
        mesh=mesh,
        in_specs=(P("tm", ("slab", "space")), P(("slab", "space"))),
        out_specs=P(("slab", "tm", "space"), None),
        check_vma=False,
    )
```

```python
import functools

import jax
import jax.numpy as jnp
from jax import lax
from jax.experimental import pallas as pl
from jax.experimental.pallas import tpu as pltpu
from jax.sharding import PartitionSpec as P

MESH = pl.DeviceIdType.MESH
LANES = 128


def shares_of(n, pieces):
    makers = n // 2 + 1
    return tuple((pieces + k) // makers for k in range(makers))


def order_of(makers):
    return list(range(makers))[1::2][::-1] + list(range(makers))[0::2][::-1]


def exchange_kernel(
    n, spaces, shares, snaps_ref, weights_ref, landed, block, stage, scale, gram,
    own_sem, ready, send_one, recv_one, send_two, recv_two,
):
    t, s = lax.axis_index("tm"), lax.axis_index("space")
    me = t * spaces + s
    makers = len(shares)
    starts = [sum(shares[:k]) for k in range(makers)]
    everyone, every_maker = n * spaces, makers * spaces
    depth = snaps_ref.shape[0]
    rows = depth // spaces
    makes = t < makers

    def device(q):
        return {"tm": q // spaces, "space": q % spaces}

    def columns(k):
        return pl.ds(starts[k] * LANES, shares[k] * LANES)

    def by_share(work):
        for share in sorted(set(shares)):
            mine = [k for k in range(makers) if shares[k] == share]
            is_mine = functools.reduce(jnp.logical_or, [t == k for k in mine])
            pl.when(is_mine)(functools.partial(work, share))

    start = sum(jnp.where(t == k, starts[k], 0) for k in range(makers))

    barrier = pltpu.get_barrier_semaphore()
    def rows_of(source, share):
        return block.at[pl.ds(pl.multiple_of(source * depth, depth), depth), pl.ds(0, share * LANES)]

    def first(k, source=snaps_ref):
        return pltpu.make_async_remote_copy(
            src_ref=source.at[:, columns(k)],
            dst_ref=rows_of(t, shares[k]),
            send_sem=send_one.at[k],
            recv_sem=recv_one.at[lax.rem(t - k + n, n)],
            device_id={"tm": k},
            device_id_type=MESH,
        )

    @pl.when(jnp.logical_not(makes))
    def _():
        pl.semaphore_wait(barrier, every_maker)
        for k in order_of(makers):
            first(k).start()

    @pl.when(makes)
    def _():
        for q in range(everyone):

            @pl.when(me != q)
            def _():
                pl.semaphore_signal(barrier, inc=1, device_id=device(q), device_id_type=MESH)

    def own(share):
        columns = pl.ds(pl.multiple_of(start * LANES, LANES), share * LANES)
        return pltpu.make_async_copy(snaps_ref.at[:, columns], rows_of(t, share), own_sem.at[0])

    load = pltpu.make_async_copy(weights_ref, scale, own_sem.at[1])
    fetch = pltpu.make_async_copy(snaps_ref, stage, own_sem.at[2])

    @by_share
    def _(share):
        fetch.start()
        own(share).start()
        load.start()


    @pl.when(makes)
    def _():
        pl.semaphore_wait(barrier, every_maker - 1)
        fetch.wait()
        for k in order_of(makers):

            @pl.when(t != k)
            def _():
                first(k, stage).start()


    for k in range(makers):
        for other in range(1, spaces):
            pl.semaphore_signal(
                ready,
                inc=1,
                device_id={"tm": k, "space": lax.rem(s + other, spaces)},
                device_id_type=MESH,
            )

    def second(q):
        return pltpu.make_async_remote_copy(
            src_ref=gram.at[pl.ds(q * rows, rows), :],
            dst_ref=landed.at[me],
            send_sem=send_two.at[q],
            recv_sem=recv_two.at[me],
            device_id=device(q),
            device_id_type=MESH,
        )

    @by_share
    def _(share):
        own(share).wait()
        load.wait()
        for d in range(1, n):
            theirs = rows_of(lax.rem(t + d, n), share)
            pltpu.make_async_copy(theirs, theirs, recv_one.at[d]).wait()
        weights = scale[pl.ds(start, share), :]
        data = block[:, 0 : share * LANES]
        weighted = jnp.concatenate(
            [data[:, k * LANES : (k + 1) * LANES] * weights[k : k + 1, :] for k in range(share)],
            axis=1,
        )
        gram[...] = lax.dot_general(
            weighted,
            data,
            (((1,), (1,)), ((), ())),
            precision=lax.Precision.HIGHEST,
            preferred_element_type=jnp.float32,
        )

    keep = pltpu.make_async_copy(
        gram.at[pl.ds(pl.multiple_of(me * rows, rows), rows), :], landed.at[jnp.where(makes, me, 0)], own_sem.at[0]
    )

    @pl.when(makes)
    def _():
        keep.start()
        pl.semaphore_wait(ready, (spaces - 1) * n)
        for q in range(everyone):

            @pl.when(me != q)
            def _():
                second(q).start()

    for m in range(every_maker):

        @pl.when(me != m)
        def _():
            pltpu.make_async_copy(landed.at[m], landed.at[m], recv_two.at[m]).wait()

    for k in range(makers):

        @pl.when(t != k)
        def _():
            first(k).wait_send()

    @pl.when(makes)
    def _():
        keep.wait()
        for q in range(everyone):

            @pl.when(me != q)
            def _():
                second(q).wait_send()


def by_exchange(n, spaces, shares, snaps, weights):
    depth, local = snaps.shape
    makers, cells = len(shares), max(shares) * LANES
    everyone, every_maker = n * spaces, makers * spaces
    order = n * depth
    rows = depth // spaces
    tiles = pl.pallas_call(
        functools.partial(exchange_kernel, n, spaces, shares),
        out_shape=jax.ShapeDtypeStruct((every_maker, rows, order), jnp.float32),
        in_specs=[pl.BlockSpec(memory_space=pl.ANY)] * 2,
        out_specs=pl.BlockSpec(memory_space=pl.ANY),
        scratch_shapes=[
            pltpu.VMEM((order, cells), jnp.float32),
            pltpu.VMEM((depth, local), jnp.float32),
            pltpu.VMEM((local // LANES, LANES), jnp.float32),
            pltpu.VMEM((order, order), jnp.float32),
            pltpu.SemaphoreType.DMA((3,)),
            pltpu.SemaphoreType.REGULAR,
            pltpu.SemaphoreType.DMA((makers,)),
            pltpu.SemaphoreType.DMA((n,)),
            pltpu.SemaphoreType.DMA((everyone,)),
            pltpu.SemaphoreType.DMA((every_maker,)),
        ],
        compiler_params=pltpu.CompilerParams(collective_id=0, has_side_effects=True),
        cost_estimate=pl.CostEstimate(
            flops=12 * order * order * cells, bytes_accessed=4 * depth * local, transcendentals=0
        ),
    )(snaps, weights.reshape(local // LANES, LANES))
    return jnp.sum(tiles, axis=0)


def from_behind(block, axis, distance):
    devices = range(lax.axis_size(axis))
    route = [((i - distance) % len(devices), i) for i in devices]
    return lax.ppermute(block, axis, route)


def by_ring(snaps, weights):
    snap_cols = snaps.shape[0]
    half_rows = snap_cols // 2
    cycle_size = lax.axis_size("tm")
    position = lax.axis_index("tm")
    halfway = cycle_size // 2
    weighted = snaps * weights[None, :]

    def product_tile(block_now):
        return lax.dot_general(
            weighted,
            block_now,
            (((1,), (1,)), ((), ())),
            precision=lax.Precision.HIGHEST,
            preferred_element_type=jnp.float32,
        )

    def advance(block_now):
        return from_behind(block_now, "tm", -1)

    partials = jnp.zeros((halfway + 1, snap_cols, snap_cols), jnp.float32)
    partials = lax.dynamic_update_index_in_dim(partials, product_tile(snaps), 0, 0)

    def advance_four(step_index, carry):
        block_now, partials = carry
        for offset_step in range(4):
            block_now = advance(block_now)
            partials = lax.dynamic_update_index_in_dim(
                partials, product_tile(block_now), 4 * step_index + offset_step + 1, 0
            )
        return (block_now, partials)

    block_now, partials = lax.fori_loop(0, halfway // 4, advance_four, (snaps, partials))
    offsets = jnp.arange(halfway + 1, dtype=jnp.int32)
    keep_last = jnp.where((offsets == halfway) & (position >= halfway), 0.0, 1.0).astype(
        jnp.float32
    )
    partials = partials * keep_last[:, None, None]
    summed = lax.psum_scatter(partials, "space", scatter_dimension=1, tiled=True)
    padding_up = jnp.zeros((cycle_size - halfway - 1, half_rows, snap_cols), jnp.float32)
    upper = jnp.roll(jnp.concatenate([summed, padding_up], axis=0), position, axis=0)
    keep_mirror = jnp.where(offsets > 0, 1.0, 0.0).astype(jnp.float32)
    flipped = jnp.swapaxes(summed, 1, 2) * keep_mirror[:, None, None]
    padding_down = jnp.zeros((cycle_size - halfway - 1, snap_cols, half_rows), jnp.float32)
    outgoing = jnp.roll(jnp.concatenate([flipped, padding_down], axis=0), position, axis=0)
    incoming = lax.all_to_all(
        lax.all_to_all(outgoing, "tm", split_axis=0, concat_axis=0, tiled=True),
        "space",
        split_axis=1,
        concat_axis=2,
        tiled=True,
    )
    panel = upper + incoming
    return jnp.transpose(panel, (1, 0, 2)).reshape(half_rows, cycle_size * snap_cols)


def solution(mesh):
    n, spaces = mesh.shape["tm"], mesh.shape["space"]

    def on_device(snaps, weights):
        depth, local = snaps.shape
        shares = shares_of(n, local // LANES)
        if local % LANES == 0 and min(shares) > 0 and depth % (8 * spaces) == 0:
            return by_exchange(n, spaces, shares, snaps, weights)
        return by_ring(snaps, weights)

    return jax.shard_map(
        on_device,
        mesh=mesh,
        in_specs=(P("tm", ("slab", "space")), P(("slab", "space"))),
        out_specs=P(("slab", "tm", "space"), None),
        check_vma=False,
    )
```

```python
import functools

import jax
import jax.numpy as jnp
from jax import lax
from jax.experimental import pallas as pl
from jax.experimental.pallas import tpu as pltpu
from jax.sharding import PartitionSpec as P

MESH = pl.DeviceIdType.MESH
LANES = 128


def shares_of(n, pieces):
    makers = n // 2 + 1
    last = min(pieces, pieces // makers + 2)
    others = [(pieces - last + k) // (makers - 1) for k in range(makers - 1)]
    return (*reversed(others), last)


def order_of(makers):
    return list(range(makers))[1::2][::-1] + list(range(makers))[0::2][::-1]


def exchange_kernel(
    n, spaces, shares, snaps_ref, weights_ref, landed, block, stage, scale, gram,
    own_sem, ready, send_one, recv_one, send_two, recv_two,
):
    t, s = lax.axis_index("tm"), lax.axis_index("space")
    me = t * spaces + s
    makers = len(shares)
    starts = [sum(shares[:k]) for k in range(makers)]
    everyone, every_maker = n * spaces, makers * spaces
    depth = snaps_ref.shape[0]
    rows = depth // spaces
    makes = t < makers

    def device(q):
        return {"tm": q // spaces, "space": q % spaces}

    def columns(k):
        return pl.ds(starts[k] * LANES, shares[k] * LANES)

    def by_share(work):
        for share in sorted(set(shares)):
            mine = [k for k in range(makers) if shares[k] == share]
            is_mine = functools.reduce(jnp.logical_or, [t == k for k in mine])
            pl.when(is_mine)(functools.partial(work, share))

    start = sum(jnp.where(t == k, starts[k], 0) for k in range(makers))

    barrier = pltpu.get_barrier_semaphore()
    def rows_of(source, share):
        return block.at[pl.ds(pl.multiple_of(source * depth, depth), depth), pl.ds(0, share * LANES)]

    def first(k, source=snaps_ref):
        return pltpu.make_async_remote_copy(
            src_ref=source.at[:, columns(k)],
            dst_ref=rows_of(t, shares[k]),
            send_sem=send_one.at[k],
            recv_sem=recv_one.at[lax.rem(t - k + n, n)],
            device_id={"tm": k},
            device_id_type=MESH,
        )

    @pl.when(jnp.logical_not(makes))
    def _():
        pl.semaphore_wait(barrier, every_maker)
        for k in order_of(makers):
            first(k).start()

    @pl.when(makes)
    def _():
        for q in range(everyone):

            @pl.when(me != q)
            def _():
                pl.semaphore_signal(barrier, inc=1, device_id=device(q), device_id_type=MESH)

    def own(share):
        columns = pl.ds(pl.multiple_of(start * LANES, LANES), share * LANES)
        return pltpu.make_async_copy(snaps_ref.at[:, columns], rows_of(t, share), own_sem.at[0])

    load = pltpu.make_async_copy(weights_ref, scale, own_sem.at[1])
    fetch = pltpu.make_async_copy(snaps_ref, stage, own_sem.at[2])

    @by_share
    def _(share):
        fetch.start()
        own(share).start()
        load.start()


    @pl.when(makes)
    def _():
        pl.semaphore_wait(barrier, every_maker - 1)
        fetch.wait()
        for k in order_of(makers):

            @pl.when(t != k)
            def _():
                first(k, stage).start()


    for k in range(makers):
        for other in range(1, spaces):
            pl.semaphore_signal(
                ready,
                inc=1,
                device_id={"tm": k, "space": lax.rem(s + other, spaces)},
                device_id_type=MESH,
            )

    def second(q):
        return pltpu.make_async_remote_copy(
            src_ref=gram.at[pl.ds(q * rows, rows), :],
            dst_ref=landed.at[me],
            send_sem=send_two.at[q],
            recv_sem=recv_two.at[me],
            device_id=device(q),
            device_id_type=MESH,
        )

    @by_share
    def _(share):
        own(share).wait()
        load.wait()
        for d in range(1, n):
            theirs = rows_of(lax.rem(t + d, n), share)
            pltpu.make_async_copy(theirs, theirs, recv_one.at[d]).wait()
        weights = scale[pl.ds(start, share), :]
        data = block[:, 0 : share * LANES]
        weighted = jnp.concatenate(
            [data[:, k * LANES : (k + 1) * LANES] * weights[k : k + 1, :] for k in range(share)],
            axis=1,
        )
        gram[...] = lax.dot_general(
            weighted,
            data,
            (((1,), (1,)), ((), ())),
            precision=lax.Precision.HIGHEST,
            preferred_element_type=jnp.float32,
        )

    keep = pltpu.make_async_copy(
        gram.at[pl.ds(pl.multiple_of(me * rows, rows), rows), :], landed.at[jnp.where(makes, me, 0)], own_sem.at[0]
    )

    @pl.when(makes)
    def _():
        keep.start()
        pl.semaphore_wait(ready, (spaces - 1) * n)
        for q in range(everyone):

            @pl.when(me != q)
            def _():
                second(q).start()

    for m in range(every_maker):

        @pl.when(me != m)
        def _():
            pltpu.make_async_copy(landed.at[m], landed.at[m], recv_two.at[m]).wait()

    for k in range(makers):

        @pl.when(t != k)
        def _():
            first(k).wait_send()

    @pl.when(makes)
    def _():
        keep.wait()
        for q in range(everyone):

            @pl.when(me != q)
            def _():
                second(q).wait_send()


def by_exchange(n, spaces, shares, snaps, weights):
    depth, local = snaps.shape
    makers, cells = len(shares), max(shares) * LANES
    everyone, every_maker = n * spaces, makers * spaces
    order = n * depth
    rows = depth // spaces
    tiles = pl.pallas_call(
        functools.partial(exchange_kernel, n, spaces, shares),
        out_shape=jax.ShapeDtypeStruct((every_maker, rows, order), jnp.float32),
        in_specs=[pl.BlockSpec(memory_space=pl.ANY)] * 2,
        out_specs=pl.BlockSpec(memory_space=pl.ANY),
        scratch_shapes=[
            pltpu.VMEM((order, cells), jnp.float32),
            pltpu.VMEM((depth, local), jnp.float32),
            pltpu.VMEM((local // LANES, LANES), jnp.float32),
            pltpu.VMEM((order, order), jnp.float32),
            pltpu.SemaphoreType.DMA((3,)),
            pltpu.SemaphoreType.REGULAR,
            pltpu.SemaphoreType.DMA((makers,)),
            pltpu.SemaphoreType.DMA((n,)),
            pltpu.SemaphoreType.DMA((everyone,)),
            pltpu.SemaphoreType.DMA((every_maker,)),
        ],
        compiler_params=pltpu.CompilerParams(collective_id=0, has_side_effects=True),
        cost_estimate=pl.CostEstimate(
            flops=12 * order * order * cells, bytes_accessed=4 * depth * local, transcendentals=0
        ),
    )(snaps, weights.reshape(local // LANES, LANES))
    return jnp.sum(tiles, axis=0)


def from_behind(block, axis, distance):
    devices = range(lax.axis_size(axis))
    route = [((i - distance) % len(devices), i) for i in devices]
    return lax.ppermute(block, axis, route)


def by_ring(snaps, weights):
    snap_cols = snaps.shape[0]
    half_rows = snap_cols // 2
    cycle_size = lax.axis_size("tm")
    position = lax.axis_index("tm")
    halfway = cycle_size // 2
    weighted = snaps * weights[None, :]

    def product_tile(block_now):
        return lax.dot_general(
            weighted,
            block_now,
            (((1,), (1,)), ((), ())),
            precision=lax.Precision.HIGHEST,
            preferred_element_type=jnp.float32,
        )

    def advance(block_now):
        return from_behind(block_now, "tm", -1)

    partials = jnp.zeros((halfway + 1, snap_cols, snap_cols), jnp.float32)
    partials = lax.dynamic_update_index_in_dim(partials, product_tile(snaps), 0, 0)

    def advance_four(step_index, carry):
        block_now, partials = carry
        for offset_step in range(4):
            block_now = advance(block_now)
            partials = lax.dynamic_update_index_in_dim(
                partials, product_tile(block_now), 4 * step_index + offset_step + 1, 0
            )
        return (block_now, partials)

    block_now, partials = lax.fori_loop(0, halfway // 4, advance_four, (snaps, partials))
    offsets = jnp.arange(halfway + 1, dtype=jnp.int32)
    keep_last = jnp.where((offsets == halfway) & (position >= halfway), 0.0, 1.0).astype(
        jnp.float32
    )
    partials = partials * keep_last[:, None, None]
    summed = lax.psum_scatter(partials, "space", scatter_dimension=1, tiled=True)
    padding_up = jnp.zeros((cycle_size - halfway - 1, half_rows, snap_cols), jnp.float32)
    upper = jnp.roll(jnp.concatenate([summed, padding_up], axis=0), position, axis=0)
    keep_mirror = jnp.where(offsets > 0, 1.0, 0.0).astype(jnp.float32)
    flipped = jnp.swapaxes(summed, 1, 2) * keep_mirror[:, None, None]
    padding_down = jnp.zeros((cycle_size - halfway - 1, snap_cols, half_rows), jnp.float32)
    outgoing = jnp.roll(jnp.concatenate([flipped, padding_down], axis=0), position, axis=0)
    incoming = lax.all_to_all(
        lax.all_to_all(outgoing, "tm", split_axis=0, concat_axis=0, tiled=True),
        "space",
        split_axis=1,
        concat_axis=2,
        tiled=True,
    )
    panel = upper + incoming
    return jnp.transpose(panel, (1, 0, 2)).reshape(half_rows, cycle_size * snap_cols)


def solution(mesh):
    n, spaces = mesh.shape["tm"], mesh.shape["space"]

    def on_device(snaps, weights):
        depth, local = snaps.shape
        shares = shares_of(n, local // LANES)
        if local % LANES == 0 and min(shares) > 0 and depth % (8 * spaces) == 0:
            return by_exchange(n, spaces, shares, snaps, weights)
        return by_ring(snaps, weights)

    return jax.shard_map(
        on_device,
        mesh=mesh,
        in_specs=(P("tm", ("slab", "space")), P(("slab", "space"))),
        out_specs=P(("slab", "tm", "space"), None),
        check_vma=False,
    )
```

```python
import functools

import jax
import jax.numpy as jnp
from jax import lax
from jax.experimental import pallas as pl
from jax.experimental.pallas import tpu as pltpu
from jax.sharding import PartitionSpec as P

MESH = pl.DeviceIdType.MESH
LANES = 128


def shares_of(n, pieces):
    makers = n // 2 + 1
    last = min(pieces, pieces // makers + 2)
    others = [(pieces - last + k) // (makers - 1) for k in range(makers - 1)]
    return (*reversed(others), last)


def order_of(makers):
    return list(range(makers))[1::2][::-1] + list(range(makers))[0::2][::-1]


def exchange_kernel(
    n, spaces, shares, snaps_ref, weights_ref, landed, block, stage, scale, gram,
    own_sem, ready, send_one, recv_one, send_two, recv_two,
):
    t, s = lax.axis_index("tm"), lax.axis_index("space")
    me = t * spaces + s
    makers = len(shares)
    starts = [sum(shares[:k]) for k in range(makers)]
    everyone, every_maker = n * spaces, makers * spaces
    depth = snaps_ref.shape[0]
    rows = depth // spaces
    makes = t < makers

    def device(q):
        return {"tm": q // spaces, "space": q % spaces}

    def columns(k):
        return pl.ds(starts[k] * LANES, shares[k] * LANES)

    def by_share(work):
        for share in sorted(set(shares)):
            mine = [k for k in range(makers) if shares[k] == share]
            is_mine = functools.reduce(jnp.logical_or, [t == k for k in mine])
            pl.when(is_mine)(functools.partial(work, share))

    start = sum(jnp.where(t == k, starts[k], 0) for k in range(makers))

    barrier = pltpu.get_barrier_semaphore()
    def rows_of(source, share):
        return block.at[pl.ds(pl.multiple_of(source * depth, depth), depth), pl.ds(0, share * LANES)]

    def first(k, source=snaps_ref):
        return pltpu.make_async_remote_copy(
            src_ref=source.at[:, columns(k)],
            dst_ref=rows_of(t, shares[k]),
            send_sem=send_one.at[k],
            recv_sem=recv_one.at[lax.rem(t - k + n, n)],
            device_id={"tm": k},
            device_id_type=MESH,
        )

    @pl.when(jnp.logical_not(makes))
    def _():
        pl.semaphore_wait(barrier, every_maker)
        for k in order_of(makers):
            pl.when(s == 0)(first(k).start)
        for k in (*range(makers - 1, 0, -2), *range(makers - 2, 0, -2), 0):
            pl.when(s > 0)(first(k).start)

    @pl.when(makes)
    def _():
        for q in range(everyone):

            @pl.when(me != q)
            def _():
                pl.semaphore_signal(barrier, inc=1, device_id=device(q), device_id_type=MESH)

    def own(share):
        columns = pl.ds(pl.multiple_of(start * LANES, LANES), share * LANES)
        return pltpu.make_async_copy(snaps_ref.at[:, columns], rows_of(t, share), own_sem.at[0])

    load = pltpu.make_async_copy(weights_ref, scale, own_sem.at[1])
    fetch = pltpu.make_async_copy(snaps_ref, stage, own_sem.at[2])

    @by_share
    def _(share):
        fetch.start()
        own(share).start()
        load.start()


    @pl.when(makes)
    def _():
        pl.semaphore_wait(barrier, every_maker - 1)
        fetch.wait()
        for k in order_of(makers):

            @pl.when(t != k)
            def _():
                first(k, stage).start()


    for k in range(makers):
        for other in range(1, spaces):
            pl.semaphore_signal(
                ready,
                inc=1,
                device_id={"tm": k, "space": lax.rem(s + other, spaces)},
                device_id_type=MESH,
            )

    def second(q):
        return pltpu.make_async_remote_copy(
            src_ref=gram.at[pl.ds(q * rows, rows), :],
            dst_ref=landed.at[me],
            send_sem=send_two.at[q],
            recv_sem=recv_two.at[me],
            device_id=device(q),
            device_id_type=MESH,
        )

    @by_share
    def _(share):
        own(share).wait()
        load.wait()
        for d in range(1, n):
            theirs = rows_of(lax.rem(t + d, n), share)
            pltpu.make_async_copy(theirs, theirs, recv_one.at[d]).wait()
        weights = scale[pl.ds(start, share), :]
        data = block[:, 0 : share * LANES]
        weighted = jnp.concatenate(
            [data[:, k * LANES : (k + 1) * LANES] * weights[k : k + 1, :] for k in range(share)],
            axis=1,
        )
        gram[...] = lax.dot_general(
            weighted,
            data,
            (((1,), (1,)), ((), ())),
            precision=lax.Precision.HIGHEST,
            preferred_element_type=jnp.float32,
        )

    keep = pltpu.make_async_copy(
        gram.at[pl.ds(pl.multiple_of(me * rows, rows), rows), :], landed.at[jnp.where(makes, me, 0)], own_sem.at[0]
    )

    @pl.when(makes)
    def _():
        keep.start()
        pl.semaphore_wait(ready, (spaces - 1) * n)
        for q in range(everyone):

            @pl.when(me != q)
            def _():
                second(q).start()

    for m in range(every_maker):

        @pl.when(me != m)
        def _():
            pltpu.make_async_copy(landed.at[m], landed.at[m], recv_two.at[m]).wait()

    for k in range(makers):

        @pl.when(t != k)
        def _():
            first(k).wait_send()

    @pl.when(makes)
    def _():
        keep.wait()
        for q in range(everyone):

            @pl.when(me != q)
            def _():
                second(q).wait_send()


def by_exchange(n, spaces, shares, snaps, weights):
    depth, local = snaps.shape
    makers, cells = len(shares), max(shares) * LANES
    everyone, every_maker = n * spaces, makers * spaces
    order = n * depth
    rows = depth // spaces
    tiles = pl.pallas_call(
        functools.partial(exchange_kernel, n, spaces, shares),
        out_shape=jax.ShapeDtypeStruct((every_maker, rows, order), jnp.float32),
        in_specs=[pl.BlockSpec(memory_space=pl.ANY)] * 2,
        out_specs=pl.BlockSpec(memory_space=pl.ANY),
        scratch_shapes=[
            pltpu.VMEM((order, cells), jnp.float32),
            pltpu.VMEM((depth, local), jnp.float32),
            pltpu.VMEM((local // LANES, LANES), jnp.float32),
            pltpu.VMEM((order, order), jnp.float32),
            pltpu.SemaphoreType.DMA((3,)),
            pltpu.SemaphoreType.REGULAR,
            pltpu.SemaphoreType.DMA((makers,)),
            pltpu.SemaphoreType.DMA((n,)),
            pltpu.SemaphoreType.DMA((everyone,)),
            pltpu.SemaphoreType.DMA((every_maker,)),
        ],
        compiler_params=pltpu.CompilerParams(collective_id=0, has_side_effects=True),
        cost_estimate=pl.CostEstimate(
            flops=12 * order * order * cells, bytes_accessed=4 * depth * local, transcendentals=0
        ),
    )(snaps, weights.reshape(local // LANES, LANES))
    return jnp.sum(tiles, axis=0)


def from_behind(block, axis, distance):
    devices = range(lax.axis_size(axis))
    route = [((i - distance) % len(devices), i) for i in devices]
    return lax.ppermute(block, axis, route)


def by_ring(snaps, weights):
    snap_cols = snaps.shape[0]
    half_rows = snap_cols // 2
    cycle_size = lax.axis_size("tm")
    position = lax.axis_index("tm")
    halfway = cycle_size // 2
    weighted = snaps * weights[None, :]

    def product_tile(block_now):
        return lax.dot_general(
            weighted,
            block_now,
            (((1,), (1,)), ((), ())),
            precision=lax.Precision.HIGHEST,
            preferred_element_type=jnp.float32,
        )

    def advance(block_now):
        return from_behind(block_now, "tm", -1)

    partials = jnp.zeros((halfway + 1, snap_cols, snap_cols), jnp.float32)
    partials = lax.dynamic_update_index_in_dim(partials, product_tile(snaps), 0, 0)

    def advance_four(step_index, carry):
        block_now, partials = carry
        for offset_step in range(4):
            block_now = advance(block_now)
            partials = lax.dynamic_update_index_in_dim(
                partials, product_tile(block_now), 4 * step_index + offset_step + 1, 0
            )
        return (block_now, partials)

    block_now, partials = lax.fori_loop(0, halfway // 4, advance_four, (snaps, partials))
    offsets = jnp.arange(halfway + 1, dtype=jnp.int32)
    keep_last = jnp.where((offsets == halfway) & (position >= halfway), 0.0, 1.0).astype(
        jnp.float32
    )
    partials = partials * keep_last[:, None, None]
    summed = lax.psum_scatter(partials, "space", scatter_dimension=1, tiled=True)
    padding_up = jnp.zeros((cycle_size - halfway - 1, half_rows, snap_cols), jnp.float32)
    upper = jnp.roll(jnp.concatenate([summed, padding_up], axis=0), position, axis=0)
    keep_mirror = jnp.where(offsets > 0, 1.0, 0.0).astype(jnp.float32)
    flipped = jnp.swapaxes(summed, 1, 2) * keep_mirror[:, None, None]
    padding_down = jnp.zeros((cycle_size - halfway - 1, snap_cols, half_rows), jnp.float32)
    outgoing = jnp.roll(jnp.concatenate([flipped, padding_down], axis=0), position, axis=0)
    incoming = lax.all_to_all(
        lax.all_to_all(outgoing, "tm", split_axis=0, concat_axis=0, tiled=True),
        "space",
        split_axis=1,
        concat_axis=2,
        tiled=True,
    )
    panel = upper + incoming
    return jnp.transpose(panel, (1, 0, 2)).reshape(half_rows, cycle_size * snap_cols)


def solution(mesh):
    n, spaces = mesh.shape["tm"], mesh.shape["space"]

    def on_device(snaps, weights):
        depth, local = snaps.shape
        shares = shares_of(n, local // LANES)
        if local % LANES == 0 and min(shares) > 0 and depth % (8 * spaces) == 0:
            return by_exchange(n, spaces, shares, snaps, weights)
        return by_ring(snaps, weights)

    return jax.shard_map(
        on_device,
        mesh=mesh,
        in_specs=(P("tm", ("slab", "space")), P(("slab", "space"))),
        out_specs=P(("slab", "tm", "space"), None),
        check_vma=False,
    )
```
